1024 devices in a mesh: island: 16 (over x, y), fsdp: 64 (over z, core).
Axes of the slice: x: 4, y: 4, z: 32, core: 2. Of those that a mesh axis runs over, the one named last changes fastest.
Arguments:
- local_params: bfloat16 [16, 64, 8192, 128], P('island', None, 'fsdp'), may hold values from -450 to 450
- global_params: float32 [64, 8192, 128], P(None, 'fsdp'), may hold values from -6 to 6
- momentum: float32 [16, 6, 8192, 128], P('island', None, 'fsdp'), may hold values from -6 to 6
- owners: int32 [64, 1], replicated, may hold values from 0 to 15; in each aligned block of 64 rows (0 to 63, 64 to 127, ...) at most 6 rows name the same one
Outputs:
- new_params: float32 [64, 8192, 128], P(None, 'fsdp')
- new_momentum: float32 [16, 6, 8192, 128], P('island', None, 'fsdp')
The draws below stay inside these ranges and needn't reach their ends.
Inputs may be any that keep to these rules, and one draw needn't show every extreme that they name: `owners`: every island owns at least one block and at most 6 blocks; some island owns exactly 6.
All inputs are finite; a program needn't handle non-finite values.
Results may differ from the reference program's by a relative error of at most 0.0028.
Values may be sent and summed in bfloat16 or wider, within the bound.
A program may use at most 64 MiB of HBM per device.

```python
import math
import jax
import jax.numpy as jnp
import numpy as np
from jax import lax

D = 8192
HD = 128
ITERS = 3
BLOCKS = 64
MOST = 6
N_ISLAND = 16


def draw_local_params(key, part):
    key = jax.random.fold_in(key, 11)
    first, second, third = jax.random.split(key, 3)
    row_scale = 3.0 ** (jnp.arange(D, dtype=jnp.float32) / D) * jnp.exp(jax.random.uniform(first, (D,), jnp.float32, 0.0, math.log(10.0)))
    col_scale = jnp.exp(jax.random.uniform(second, (HD,), jnp.float32, 0.0, math.log(10.0)))
    noise = jnp.clip(jax.random.normal(third, (N_ISLAND, BLOCKS, D, HD), jnp.float32), -4.0, 4.0)
    values = 0.3 * noise * row_scale[None, None, :, None] * col_scale[None, None, None, :]
    return values.astype(jnp.bfloat16)


def shard_levels(stream_key, dims, pieces, low, largest):
    def one(axis_at, parts):
        steps = jax.random.uniform(jax.random.fold_in(jax.random.fold_in(stream_key, 6), axis_at), (parts,), jnp.float32, low / len(pieces), largest / len(pieces))
        return jnp.repeat(jnp.exp(steps), dims[axis_at] // parts).reshape((-1,) + (1,) * (len(dims) - axis_at - 1))

    gain = one(*pieces[0])
    for cut in pieces[1:]:
        gain = gain * one(*cut)
    return gain


def assign_block(stream_key, own, number, rows, amount, top, most, slope):
    order = jax.random.permutation(stream_key, amount)
    heavy_load, ordinary = shares(amount, rows * top, most, slope, True), shares(amount, rows * top, most, slope, False)
    places = jnp.arange(amount)

    def named(tallies, offset_by):
        used = int((tallies > 0).sum())
        fixed = max(1, used // 4)
        shifted = fixed + (places - fixed + offset_by * (used - fixed)) % max(1, amount - fixed)
        return jnp.zeros((amount,), jnp.int32).at[order[jnp.where(places < fixed, places, shifted)]].set(jnp.asarray(tallies, jnp.int32))

    tallies = jnp.where(number % 4 == 0, named(heavy_load, number // 4), named(ordinary, number - number // 4 - 1))
    mixed = jax.random.permutation(jax.random.fold_in(own, 3), amount)
    source_of, sink = mixed[0:amount // 2 * 2:2], mixed[1:amount // 2 * 2:2]
    slack = jnp.minimum(tallies[source_of] - 1, most - tallies[sink]) // 2
    slack = jnp.where((source_of == order[0]) | (sink == order[0]) | (tallies[sink] == 0), 0, jnp.maximum(slack, 0))
    shifted = jax.random.randint(jax.random.fold_in(own, 4), (amount // 2,), 0, 1 << 20) % (slack + 1)
    tallies = tallies.at[source_of].add(-shifted).at[sink].add(shifted)
    items = jnp.searchsorted(jnp.cumsum(tallies), jnp.arange(rows * top), side="right").astype(jnp.int32)
    listing = items.reshape(top, rows).T
    listing = listing[jax.random.permutation(jax.random.fold_in(own, 1), rows)]
    offset_by = jax.random.randint(jax.random.fold_in(own, 2), (rows, 1), 0, top)
    return jnp.take_along_axis(listing, (jnp.arange(top)[None, :] + offset_by) % top, axis=1)


def shares(number_of, total, bound, lean, full):
    portions = [(1 << 20) // math.isqrt(grade ** lean) + 1 for grade in range(1, number_of + 1)]
    largest = bound if full else min(bound, max(-(-total // number_of), total * portions[0] // sum(portions)))
    least = 1 if total - largest >= number_of - 1 else 0
    counts, spare = [largest] + [least] * (number_of - 1), total - largest - least * (number_of - 1)
    while spare > 0:
        movable = [i for i in range(1, number_of) if counts[i] < largest] or [i for i in range(1, number_of) if counts[i] < bound]
        pool, budget = sum([portions[i] for i in movable]), spare
        for i in movable:
            more = min(bound - counts[i], max(1, budget * portions[i] // pool), spare)
            counts[i] = counts[i] + more
            spare = spare - more
    return np.array(counts)


def gaussian(stream_key, shape, scale, reach, pieces=(), kind=jnp.bfloat16):
    array = jax.random.normal(stream_key, shape, jnp.float32) * scale
    if len(pieces) > 0:
        array = shard_levels(stream_key, shape, pieces, -0.22, 0.18) * array
    return jnp.clip(array, min=-reach, max=reach).astype(kind)


def setup_inputs(seed: int = 0) -> dict:
    seeds = jax.random.split(jax.random.key(seed), 5)
    local_params = draw_local_params(jax.random.fold_in(seeds[4], 71), 0)
    global_params = gaussian(seeds[1], (BLOCKS, D, HD), 1.0, 6.0, ((1, 64),), jnp.float32)
    momentum = gaussian(seeds[2], (N_ISLAND, MOST, D, HD), 1.0, 6.0, ((0, 16), (2, 64)), jnp.float32)
    owners_keys = jax.random.split(jax.random.fold_in(seeds[3], 1), BLOCKS // BLOCKS)
    owners_turns = jax.random.permutation(jax.random.fold_in(seeds[3], 3), BLOCKS // BLOCKS)
    owners = jax.vmap(lambda own, number: assign_block(jax.random.fold_in(seeds[3], 2), own, number, BLOCKS, N_ISLAND, 1, MOST, 2))(owners_keys, owners_turns).reshape((BLOCKS, 1))
    return {"local_params": local_params, "global_params": global_params, "momentum": momentum, "owners": owners}


decay_rate = 0.9
epsilon_norm = 1e-07
coef_a = 3.4445
coef_b = -4.775
coef_c = 2.0315

def slot_table(owner_list, islands, slots):
    onehot = (owner_list[:, None] == jnp.arange(islands, dtype=jnp.int32)[None, :]).astype(jnp.int32)
    earlier = jnp.cumsum(onehot, axis=0) - onehot
    position = lax.optimization_barrier(jnp.sum(earlier * onehot, axis=1))
    target = owner_list * slots + position
    return (jnp.arange(islands * slots, dtype=jnp.int32)[:, None] == target[None, :]).astype(jnp.float32)

def reference(local_params, global_params, momentum, owners):
    table = slot_table(owners[:, 0].astype(jnp.int32), N_ISLAND, MOST)
    total = jnp.zeros(global_params.shape, jnp.float32)
    for island_index in range(N_ISLAND):
        total = total + (global_params - local_params[island_index].astype(jnp.float32))
    pseudo = (total / N_ISLAND).astype(jnp.bfloat16)
    pseudo = lax.optimization_barrier(pseudo).astype(jnp.float32)
    gathered = jnp.dot(table, pseudo.reshape(BLOCKS, D * HD), precision=lax.Precision.HIGHEST)
    gathered = gathered.reshape(N_ISLAND * MOST, D, HD)
    used = (lax.optimization_barrier(jnp.sum(table, axis=1)) > 0.5)[:, None, None]
    previous = momentum.reshape(N_ISLAND * MOST, D, HD)
    new_momentum = jnp.where(used, decay_rate * previous + gathered, previous)
    looking = jnp.where(used, gathered + decay_rate * new_momentum, jnp.float32(0.0))
    squares = lax.optimization_barrier(jnp.sum(looking * looking, axis=(1, 2)))
    iterate = looking / (jnp.sqrt(squares) + epsilon_norm)[:, None, None]
    for repeat in range(ITERS):
        gram = jnp.einsum('srh,srk->shk', iterate, iterate, precision=lax.Precision.HIGHEST)
        poly = coef_b * gram + coef_c * jnp.einsum('shk,skj->shj', gram, gram, precision=lax.Precision.HIGHEST)
        iterate = coef_a * iterate + jnp.einsum('srh,shk->srk', iterate, poly, precision=lax.Precision.HIGHEST)
    update = jnp.dot(table.T, iterate.reshape(N_ISLAND * MOST, D * HD), precision=lax.Precision.HIGHEST)
    new_params = global_params - math.sqrt(D / HD) * update.reshape(BLOCKS, D, HD)
    return (new_params, new_momentum.reshape(N_ISLAND, MOST, D, HD))
```

```python
import math

import jax
import jax.numpy as jnp
from jax import lax
from jax.experimental import pallas as pl
from jax.experimental.pallas import tpu as pltpu
from jax.sharding import PartitionSpec as P

MESH = pl.DeviceIdType.MESH
HIGHEST = lax.Precision.HIGHEST
decay_rate = 0.9
epsilon_norm = 1e-07
coef_a = 3.4445
coef_b = -4.775
coef_c = 2.0315

N = 4
NEAR = 4
FAR = 8
HALF = 64
LOOK_P = 1.0 + decay_rate
LOOK_M = decay_rate * decay_rate


def kernel(
    table, local, globe, mom, xall, newmom,
    lown, g_a, g_b, r1a, r1b, s2a, s2b, r2a, r2b, look, lookall, gpart, gsend, rnear, fown, rfar, gfull,
    load_sem, g_sem, s1_send, s1_recv, s2_send, s2_recv,
    l_send, l_recv, lf_send, lf_recv, x_send, x_recv, xf_send, xf_recv, n_send, n_recv, f_send, f_recv, a_send, a_recv,
):
    island, fsdp = lax.axis_index("island"), lax.axis_index("fsdp")
    x, y = island // N, island % N
    z, core = fsdp // 2, fsdp % 2
    near = (z % NEAR) * 2 + core

    def at_xy(px, py):
        return (px * N + py, fsdp)

    def x_peer(j):
        return at_xy((x + j) % N, y)

    def y_peer(j):
        return at_xy(x, (y + j) % N)

    def near_peer(q):
        other = (near + q) % (2 * NEAR)
        return (island, ((z // NEAR) * NEAR + other // 2) * 2 + other % 2)

    def far_peer(q):
        return (island, ((z + NEAR * q) % (NEAR * FAR)) * 2 + core)

    barrier = pltpu.get_barrier_semaphore()
    peers = [x_peer(j) for j in range(1, N)] + [y_peer(j) for j in range(1, N)]
    peers += [near_peer(q) for q in range(1, 2 * NEAR)] + [far_peer(q) for q in range(1, FAR)]
    for peer in peers:
        pl.semaphore_signal(barrier, inc=1, device_id=peer, device_id_type=MESH)

    order = [(t, j) for t in (1, 2, 3, 0) for j in (1, 2, 3, 0)]
    loads = {}
    for t, j in order:
        place = ((x + t) % N, (y + j) % N)
        loads[t, j] = pltpu.make_async_copy(local.at[place], lown.at[place], load_sem.at[t * N + j])
        loads[t, j].start()
    load_a = pltpu.make_async_copy(globe.at[:, y, :, 0:HALF, :], g_a, g_sem.at[0])
    load_b = pltpu.make_async_copy(globe.at[x, :, :, HALF : 2 * HALF, :], g_b, g_sem.at[1])
    load_a.start()
    load_b.start()
    pl.semaphore_wait(barrier, len(peers))

    def remote(src, dst, send, recv, peer):
        return pltpu.make_async_remote_copy(
            src_ref=src, dst_ref=dst, send_sem=send, recv_sem=recv, device_id=peer, device_id_type=MESH
        )

    sent = []
    first_a, first_b = {}, {}
    inject = 16.0 * LOOK_M / LOOK_P
    for t, j in order:
        px, py = (x + t) % N, (y + j) % N
        loads[t, j].wait()

        def put(k, _, px=px, py=py):
            block = (px * N + py) * N + k
            scale = table[64 + block].astype(jnp.float32) * inject
            term = lown[px, py, k].astype(jnp.float32) - scale * mom[table[block]]
            lown[px, py, k] = term.astype(jnp.bfloat16)
            return 0

        lax.fori_loop(0, N, put, 0)
        if j:
            at = (j - 1) * N + t
            copy = remote(
                lown.at[px, py, :, 0:HALF, :], r1a.at[j - 1, px], s1_send.at[0, at], s1_recv.at[0, at], y_peer(j)
            )
            copy.start()
            first_a[t, j] = copy
        if t:
            at = (t - 1) * N + j
            copy = remote(
                lown.at[px, py, :, HALF : 2 * HALF, :], r1b.at[t - 1, py], s1_send.at[1, at], s1_recv.at[1, at], x_peer(t)
            )
            copy.start()
            first_b[t, j] = copy
    sent += list(first_a.values()) + list(first_b.values())
    load_a.wait()
    load_b.wait()

    def line_a(t):
        px = (x + t) % N
        for j in range(1, N):
            first_a[t, j].wait_recv()
        total = lown[px, y, :, 0:HALF, :].astype(jnp.float32)
        for j in range(1, N):
            total = total + r1a[j - 1, px].astype(jnp.float32)
        return N * g_a[px] - total

    def line_b(j):
        py = (y + j) % N
        for t in range(1, N):
            first_b[t, j].wait_recv()
        total = lown[x, py, :, HALF : 2 * HALF, :].astype(jnp.float32)
        for t in range(1, N):
            total = total + r1b[t - 1, py].astype(jnp.float32)
        return N * g_b[py] - total

    second = []
    for s in range(1, N):
        s2a[s - 1] = line_a(s).astype(jnp.bfloat16)
        copy_a = remote(s2a.at[s - 1], r2a.at[s - 1], s2_send.at[0, s - 1], s2_recv.at[0, s - 1], x_peer(s))
        copy_a.start()
        s2b[s - 1] = line_b(s).astype(jnp.bfloat16)
        copy_b = remote(s2b.at[s - 1], r2b.at[s - 1], s2_send.at[1, s - 1], s2_recv.at[1, s - 1], y_peer(s))
        copy_b.start()
        second += [copy_a, copy_b]
    look[:, 0:HALF, :] = line_a(0)
    look[:, HALF : 2 * HALF, :] = line_b(0)
    for copy in second:
        copy.wait_recv()
    sent += second
    total_a, total_b = look[:, 0:HALF, :], look[:, HALF : 2 * HALF, :]
    for s in range(N - 1):
        total_a = total_a + r2a[s].astype(jnp.float32)
        total_b = total_b + r2b[s].astype(jnp.float32)
    look[:, 0:HALF, :] = total_a * (LOOK_P / 16.0)
    look[:, HALF : 2 * HALF, :] = total_b * (LOOK_P / 16.0)
    lookall[x, y] = look[...].astype(jnp.bfloat16)

    def gather_own(buf, send, recv):
        copies = []
        for j in range(1, N):
            for way, peer in enumerate((x_peer(j), y_peer(j))):
                copy = remote(buf.at[x, y], buf.at[x, y], send.at[way, j - 1], recv.at[way, j - 1], peer)
                copy.start()
                copies.append(copy)
        return copies

    def gather_forward(buf, direct, send, recv):
        copies = []
        for j in range(1, N):
            for way in range(2):
                direct[(j - 1) * 2 + way].wait_recv()
                for i in range(1, N):
                    at = (j - 1) * (N - 1) + i - 1
                    if way == 0:
                        piece = buf.at[(x - j + N) % N, y, :, 0:HALF, :]
                        copy = remote(piece, piece, send.at[0, at], recv.at[0, at], y_peer(i))
                    else:
                        piece = buf.at[x, (y - j + N) % N, :, HALF : 2 * HALF, :]
                        copy = remote(piece, piece, send.at[1, at], recv.at[1, at], x_peer(i))
                    copy.start()
                    copies.append(copy)
        return copies

    look_direct = gather_own(lookall, l_send, l_recv)
    sent += look_direct

    for k in range(N):
        block = look[k]
        gram = lax.dot_general(
            block, block, (((0,), (0,)), ((), ())), precision=HIGHEST, preferred_element_type=jnp.float32
        )
        gpart[2 * k] = gram[0:HALF]
        gpart[2 * k + 1] = gram[HALF : 2 * HALF]
    gsend[...] = gpart[...].astype(jnp.bfloat16)
    steps = []
    for q in range(1, 2 * NEAR):
        other = (near + q) % (2 * NEAR)
        copy = remote(gsend.at[other], rnear.at[q - 1], n_send.at[q - 1], n_recv.at[q - 1], near_peer(q))
        copy.start()
        steps.append(copy)
    for copy in steps:
        copy.wait_recv()
    sent += steps
    mine = gpart[near]
    for q in range(2 * NEAR - 1):
        mine = mine + rnear[q].astype(jnp.float32)
    fown[...] = mine.astype(jnp.bfloat16)
    steps = []
    for q in range(1, FAR):
        copy = remote(fown, rfar.at[q - 1], f_send.at[q - 1], f_recv.at[q - 1], far_peer(q))
        copy.start()
        steps.append(copy)
    look_forward = gather_forward(lookall, look_direct, lf_send, lf_recv)
    sent += look_forward
    for copy in steps:
        copy.wait_recv()
    sent += steps
    for q in range(FAR - 1):
        mine = mine + rfar[q].astype(jnp.float32)
    gfull[near] = mine.astype(jnp.bfloat16)
    steps = []
    for q in range(1, 2 * NEAR):
        copy = remote(gfull.at[near], gfull.at[near], a_send.at[q - 1], a_recv.at[q - 1], near_peer(q))
        copy.start()
        steps.append(copy)
    for copy in steps:
        copy.wait_recv()
    sent += steps

    def mm(left, right):
        return jnp.dot(left, right, precision=HIGHEST, preferred_element_type=jnp.float32)

    rows = lax.broadcasted_iota(jnp.int32, (2 * HALF, 2 * HALF), 0)
    cols = lax.broadcasted_iota(jnp.int32, (2 * HALF, 2 * HALF), 1)
    eye = jnp.where(rows == cols, 1.0, 0.0).astype(jnp.float32)
    grams, scales = [], []
    for k in range(N):
        gram = gfull[2 * k : 2 * k + 2].astype(jnp.float32).reshape(2 * HALF, 2 * HALF)
        squares = jnp.sum(jnp.sum(gram * eye, axis=1, keepdims=True), axis=0, keepdims=True)
        scale = 1.0 / (jnp.sqrt(squares) + epsilon_norm)
        grams.append(gram * scale * scale)
        scales.append(scale)
    mults = None
    for step in range(3):
        squared = [mm(gram, gram) for gram in grams]
        polys = [coef_a * eye + coef_b * gram + coef_c * square for gram, square in zip(grams, squared)]
        if step < 2:
            inner = [mm(poly, gram) for poly, gram in zip(polys, grams)]
            grams = [mm(poly, part) for poly, part in zip(polys, inner)]
        mults = polys if mults is None else [mm(mult, poly) for mult, poly in zip(mults, polys)]
    for k in range(N):
        xall[x, y, k] = mm(look[k], mults[k] * scales[k]).astype(jnp.bfloat16)

    x_direct = gather_own(xall, x_send, x_recv)
    sent += x_direct

    for copy in look_forward:
        copy.wait_recv()

    for s in range(newmom.shape[0]):
        block = table[128 + s]
        used = table[136 + s]
        old = mom[s]
        seen = lookall[block // 16, (block // N) % N, block % N].astype(jnp.float32)
        fresh = decay_rate * old + (seen - LOOK_M * old) * (1.0 / LOOK_P)
        newmom[s] = jnp.where(used > 0, fresh, old)

    x_forward = gather_forward(xall, x_direct, xf_send, xf_recv)
    sent += x_forward
    for copy in x_forward:
        copy.wait_recv()
    for copy in sent:
        copy.wait_send()


def shards(local_params, global_params, momentum, owners):
    my_island = lax.axis_index("island")
    blocks, height, width = global_params.shape
    slots = momentum.shape[1]
    owner = owners[:, 0]
    ids = jnp.arange(blocks, dtype=jnp.int32)
    earlier = (owner[None, :] == owner[:, None]) & (ids[None, :] < ids[:, None])
    position = jnp.sum(earlier.astype(jnp.int32), axis=1)
    own = owner == my_island
    route = jnp.where(own, position, 0)
    hit = own[None, :] & (position[None, :] == jnp.arange(8, dtype=jnp.int32)[:, None])
    holds = jnp.sum(jnp.where(hit, ids[None, :], 0), axis=1)
    used = jnp.sum(hit.astype(jnp.int32), axis=1)
    table = jnp.concatenate([route, own.astype(jnp.int32), holds, used])

    bf, f4 = jnp.bfloat16, jnp.float32
    dma = pltpu.SemaphoreType.DMA
    vmem = pltpu.VMEM
    gathered, new_momentum = pl.pallas_call(
        kernel,
        out_shape=(
            jax.ShapeDtypeStruct((N, N, N, height, width), bf),
            jax.ShapeDtypeStruct((slots, height, width), f4),
        ),
        in_specs=[
            pl.BlockSpec(memory_space=pltpu.SMEM),
            pl.BlockSpec(memory_space=pl.ANY),
            pl.BlockSpec(memory_space=pl.ANY),
            pl.BlockSpec(memory_space=vmem),
        ],
        out_specs=(pl.BlockSpec(memory_space=vmem), pl.BlockSpec(memory_space=vmem)),
        scratch_shapes=[
            vmem((N, N, N, height, width), bf),
            vmem((N, N, HALF, width), f4),
            vmem((N, N, HALF, width), f4),
            vmem((N - 1, N, N, HALF, width), bf),
            vmem((N - 1, N, N, HALF, width), bf),
            vmem((N - 1, N, HALF, width), bf),
            vmem((N - 1, N, HALF, width), bf),
            vmem((N - 1, N, HALF, width), bf),
            vmem((N - 1, N, HALF, width), bf),
            vmem((N, height, width), f4),
            vmem((N, N, N, height, width), bf),
            vmem((2 * N, HALF, width), f4),
            vmem((2 * N, HALF, width), bf),
            vmem((2 * NEAR - 1, HALF, width), bf),
            vmem((HALF, width), bf),
            vmem((FAR - 1, HALF, width), bf),
            vmem((2 * N, HALF, width), bf),
            dma((N * N,)),
            dma((2,)),
            dma((2, (N - 1) * N)),
            dma((2, (N - 1) * N)),
            dma((2, N - 1)),
            dma((2, N - 1)),
            dma((2, N - 1)),
            dma((2, N - 1)),
            dma((2, (N - 1) * (N - 1))),
            dma((2, (N - 1) * (N - 1))),
            dma((2, N - 1)),
            dma((2, N - 1)),
            dma((2, (N - 1) * (N - 1))),
            dma((2, (N - 1) * (N - 1))),
            dma((2 * NEAR - 1,)),
            dma((2 * NEAR - 1,)),
            dma((FAR - 1,)),
            dma((FAR - 1,)),
            dma((2 * NEAR - 1,)),
            dma((2 * NEAR - 1,)),
        ],
        compiler_params=pltpu.CompilerParams(
            collective_id=0, has_side_effects=True, vmem_limit_bytes=32 * 1024 * 1024
        ),
        name="outer_step",
    )(
        table,
        local_params.reshape(N, N, N, height, width),
        global_params.reshape(N, N, N, height, width),
        momentum[0],
    )
    factor = math.sqrt(height * lax.axis_size("fsdp") / width)
    update = gathered.reshape(blocks, height, width).astype(f4)
    return (global_params - factor * update, new_momentum[None])


def solution(mesh):
    in_specs = (
        P("island", None, "fsdp", None),
        P(None, "fsdp", None),
        P("island", None, "fsdp", None),
        P(),
    )
    out_specs = (P(None, "fsdp", None), P("island", None, "fsdp", None))
    return jax.shard_map(shards, mesh=mesh, in_specs=in_specs, out_specs=out_specs, check_vma=False)
```

```python
import math

import jax
import jax.numpy as jnp
from jax import lax
from jax.experimental import pallas as pl
from jax.experimental.pallas import tpu as pltpu
from jax.sharding import PartitionSpec as P

MESH = pl.DeviceIdType.MESH
HIGHEST = lax.Precision.HIGHEST
decay_rate = 0.9
epsilon_norm = 1e-07
coef_a = 3.4445
coef_b = -4.775
coef_c = 2.0315

N = 4
NEAR = 4
FAR = 8
HALF = 64
LOOK_P = 1.0 + decay_rate
LOOK_M = decay_rate * decay_rate


def kernel(
    table, local, globe, mom, xall, newmom,
    lown, g_a, g_b, r1a, r1b, s2a, s2b, r2a, r2b, look, lookall, gpart, gsend, rnear, fown, rfar, gfull,
    load_sem, g_sem, s1_send, s1_recv, s2_send, s2_recv,
    l_send, l_recv, lf_send, lf_recv, x_send, x_recv, xf_send, xf_recv, n_send, n_recv, f_send, f_recv, a_send, a_recv,
):
    island, fsdp = lax.axis_index("island"), lax.axis_index("fsdp")
    x, y = island // N, island % N
    z, core = fsdp // 2, fsdp % 2
    near = (z % NEAR) * 2 + core

    def at_xy(px, py):
        return (px * N + py, fsdp)

    def x_peer(j):
        return at_xy((x + j) % N, y)

    def y_peer(j):
        return at_xy(x, (y + j) % N)

    def near_peer(q):
        other = (near + q) % (2 * NEAR)
        return (island, ((z // NEAR) * NEAR + other // 2) * 2 + other % 2)

    def far_peer(q):
        return (island, ((z + NEAR * q) % (NEAR * FAR)) * 2 + core)

    barrier = pltpu.get_barrier_semaphore()
    peers = [x_peer(j) for j in range(1, N)] + [y_peer(j) for j in range(1, N)]
    peers += [near_peer(q) for q in range(1, 2 * NEAR)] + [far_peer(q) for q in (1, 2, FAR - 2, FAR - 1)]
    for peer in peers:
        pl.semaphore_signal(barrier, inc=1, device_id=peer, device_id_type=MESH)

    order = [(t, j) for t in (1, 2, 3, 0) for j in (1, 2, 3, 0)]
    loads = {}
    for t, j in order:
        place = ((x + t) % N, (y + j) % N)
        loads[t, j] = pltpu.make_async_copy(local.at[place], lown.at[place], load_sem.at[t * N + j])
        loads[t, j].start()
    load_a = pltpu.make_async_copy(globe.at[:, y, :, 0:HALF, :], g_a, g_sem.at[0])
    load_b = pltpu.make_async_copy(globe.at[x, :, :, HALF : 2 * HALF, :], g_b, g_sem.at[1])
    load_a.start()
    load_b.start()
    pl.semaphore_wait(barrier, len(peers))

    def remote(src, dst, send, recv, peer):
        return pltpu.make_async_remote_copy(
            src_ref=src, dst_ref=dst, send_sem=send, recv_sem=recv, device_id=peer, device_id_type=MESH
        )

    sent = []
    first_a, first_b = {}, {}
    inject = 16.0 * LOOK_M / LOOK_P
    for t, j in order:
        px, py = (x + t) % N, (y + j) % N
        loads[t, j].wait()

        def put(k, _, px=px, py=py):
            block = (px * N + py) * N + k
            scale = table[64 + block].astype(jnp.float32) * inject
            term = lown[px, py, k].astype(jnp.float32) - scale * mom[table[block]]
            lown[px, py, k] = term.astype(jnp.bfloat16)
            return 0

        lax.fori_loop(0, N, put, 0)
        if j:
            at = (j - 1) * N + t
            copy = remote(
                lown.at[px, py, :, 0:HALF, :], r1a.at[j - 1, px], s1_send.at[0, at], s1_recv.at[0, at], y_peer(j)
            )
            copy.start()
            first_a[t, j] = copy
        if t:
            at = (t - 1) * N + j
            copy = remote(
                lown.at[px, py, :, HALF : 2 * HALF, :], r1b.at[t - 1, py], s1_send.at[1, at], s1_recv.at[1, at], x_peer(t)
            )
            copy.start()
            first_b[t, j] = copy
    sent += list(first_a.values()) + list(first_b.values())
    load_a.wait()
    load_b.wait()

    def line_a(t):
        px = (x + t) % N
        for j in range(1, N):
            first_a[t, j].wait_recv()
        total = lown[px, y, :, 0:HALF, :].astype(jnp.float32)
        for j in range(1, N):
            total = total + r1a[j - 1, px].astype(jnp.float32)
        return N * g_a[px] - total

    def line_b(j):
        py = (y + j) % N
        for t in range(1, N):
            first_b[t, j].wait_recv()
        total = lown[x, py, :, HALF : 2 * HALF, :].astype(jnp.float32)
        for t in range(1, N):
            total = total + r1b[t - 1, py].astype(jnp.float32)
        return N * g_b[py] - total

    second = []
    for s in range(1, N):
        s2a[s - 1] = line_a(s).astype(jnp.bfloat16)
        copy_a = remote(s2a.at[s - 1], r2a.at[s - 1], s2_send.at[0, s - 1], s2_recv.at[0, s - 1], x_peer(s))
        copy_a.start()
        s2b[s - 1] = line_b(s).astype(jnp.bfloat16)
        copy_b = remote(s2b.at[s - 1], r2b.at[s - 1], s2_send.at[1, s - 1], s2_recv.at[1, s - 1], y_peer(s))
        copy_b.start()
        second += [copy_a, copy_b]
    look[:, 0:HALF, :] = line_a(0)
    look[:, HALF : 2 * HALF, :] = line_b(0)
    for copy in second:
        copy.wait_recv()
    sent += second
    total_a, total_b = look[:, 0:HALF, :], look[:, HALF : 2 * HALF, :]
    for s in range(N - 1):
        total_a = total_a + r2a[s].astype(jnp.float32)
        total_b = total_b + r2b[s].astype(jnp.float32)
    look[:, 0:HALF, :] = total_a * (LOOK_P / 16.0)
    look[:, HALF : 2 * HALF, :] = total_b * (LOOK_P / 16.0)
    lookall[x, y] = look[...].astype(jnp.bfloat16)

    def gather_own(buf, send, recv):
        copies = []
        for j in range(1, N):
            for way, peer in enumerate((x_peer(j), y_peer(j))):
                copy = remote(buf.at[x, y], buf.at[x, y], send.at[way, j - 1], recv.at[way, j - 1], peer)
                copy.start()
                copies.append(copy)
        return copies

    def gather_forward(buf, direct, send, recv):
        copies = []
        for j in range(1, N):
            for way in range(2):
                direct[(j - 1) * 2 + way].wait_recv()
                for i in range(1, N):
                    at = (j - 1) * (N - 1) + i - 1
                    if way == 0:
                        piece = buf.at[(x - j + N) % N, y, :, 0:HALF, :]
                        copy = remote(piece, piece, send.at[0, at], recv.at[0, at], y_peer(i))
                    else:
                        piece = buf.at[x, (y - j + N) % N, :, HALF : 2 * HALF, :]
                        copy = remote(piece, piece, send.at[1, at], recv.at[1, at], x_peer(i))
                    copy.start()
                    copies.append(copy)
        return copies

    look_direct = gather_own(lookall, l_send, l_recv)
    sent += look_direct

    for k in range(N):
        block = look[k]
        gram = lax.dot_general(
            block, block, (((0,), (0,)), ((), ())), precision=HIGHEST, preferred_element_type=jnp.float32
        )
        gpart[2 * k] = gram[0:HALF]
        gpart[2 * k + 1] = gram[HALF : 2 * HALF]
    gsend[...] = gpart[...].astype(jnp.bfloat16)
    steps = []
    for q in range(1, 2 * NEAR):
        other = (near + q) % (2 * NEAR)
        copy = remote(gsend.at[other], rnear.at[q - 1], n_send.at[q - 1], n_recv.at[q - 1], near_peer(q))
        copy.start()
        steps.append(copy)
    for copy in steps:
        copy.wait_recv()
    sent += steps
    mine = gpart[near]
    for q in range(2 * NEAR - 1):
        mine = mine + rnear[q].astype(jnp.float32)
    fown[...] = mine.astype(jnp.bfloat16)
    steps = []
    for slot, q in enumerate((2, FAR - 2, 1, FAR - 1)):
        copy = remote(fown, rfar.at[slot], f_send.at[slot], f_recv.at[slot], far_peer(q))
        copy.start()
        steps.append(copy)
    steps[0].wait_recv()
    for slot, q in ((4, 2), (5, 1)):
        copy = remote(rfar.at[0], rfar.at[slot], f_send.at[slot], f_recv.at[slot], far_peer(q))
        copy.start()
        steps.append(copy)
    steps[1].wait_recv()
    copy = remote(rfar.at[1], rfar.at[6], f_send.at[6], f_recv.at[6], far_peer(FAR - 1))
    copy.start()
    steps.append(copy)
    look_forward = gather_forward(lookall, look_direct, lf_send, lf_recv)
    sent += look_forward
    for copy in steps[2:]:
        copy.wait_recv()
    sent += steps
    for q in range(FAR - 1):
        mine = mine + rfar[q].astype(jnp.float32)
    gfull[near] = mine.astype(jnp.bfloat16)
    steps = []
    for q in range(1, 2 * NEAR):
        copy = remote(gfull.at[near], gfull.at[near], a_send.at[q - 1], a_recv.at[q - 1], near_peer(q))
        copy.start()
        steps.append(copy)
    for copy in steps:
        copy.wait_recv()
    sent += steps

    def mm(left, right):
        return jnp.dot(left, right, precision=HIGHEST, preferred_element_type=jnp.float32)

    rows = lax.broadcasted_iota(jnp.int32, (2 * HALF, 2 * HALF), 0)
    cols = lax.broadcasted_iota(jnp.int32, (2 * HALF, 2 * HALF), 1)
    eye = jnp.where(rows == cols, 1.0, 0.0).astype(jnp.float32)
    grams, scales = [], []
    for k in range(N):
        gram = gfull[2 * k : 2 * k + 2].astype(jnp.float32).reshape(2 * HALF, 2 * HALF)
        squares = jnp.sum(jnp.sum(gram * eye, axis=1, keepdims=True), axis=0, keepdims=True)
        scale = 1.0 / (jnp.sqrt(squares) + epsilon_norm)
        grams.append(gram * scale * scale)
        scales.append(scale)
    mults = None
    for step in range(3):
        squared = [mm(gram, gram) for gram in grams]
        polys = [coef_a * eye + coef_b * gram + coef_c * square for gram, square in zip(grams, squared)]
        if step < 2:
            inner = [mm(poly, gram) for poly, gram in zip(polys, grams)]
            grams = [mm(poly, part) for poly, part in zip(polys, inner)]
        mults = polys if mults is None else [mm(mult, poly) for mult, poly in zip(mults, polys)]
    for k in range(N):
        xall[x, y, k] = mm(look[k], mults[k] * scales[k]).astype(jnp.bfloat16)

    x_direct = gather_own(xall, x_send, x_recv)
    sent += x_direct

    for copy in look_forward:
        copy.wait_recv()

    for s in range(newmom.shape[0]):
        block = table[128 + s]
        used = table[136 + s]
        old = mom[s]
        seen = lookall[block // 16, (block // N) % N, block % N].astype(jnp.float32)
        fresh = decay_rate * old + (seen - LOOK_M * old) * (1.0 / LOOK_P)
        newmom[s] = jnp.where(used > 0, fresh, old)

    x_forward = gather_forward(xall, x_direct, xf_send, xf_recv)
    sent += x_forward
    for copy in x_forward:
        copy.wait_recv()
    for copy in sent:
        copy.wait_send()


def shards(local_params, global_params, momentum, owners):
    my_island = lax.axis_index("island")
    blocks, height, width = global_params.shape
    slots = momentum.shape[1]
    owner = owners[:, 0]
    ids = jnp.arange(blocks, dtype=jnp.int32)
    earlier = (owner[None, :] == owner[:, None]) & (ids[None, :] < ids[:, None])
    position = jnp.sum(earlier.astype(jnp.int32), axis=1)
    own = owner == my_island
    route = jnp.where(own, position, 0)
    hit = own[None, :] & (position[None, :] == jnp.arange(8, dtype=jnp.int32)[:, None])
    holds = jnp.sum(jnp.where(hit, ids[None, :], 0), axis=1)
    used = jnp.sum(hit.astype(jnp.int32), axis=1)
    table = jnp.concatenate([route, own.astype(jnp.int32), holds, used])

    def in_hbm(array):
        return pltpu.with_memory_space_constraint(array, pltpu.HBM)

    bf, f4 = jnp.bfloat16, jnp.float32
    dma = pltpu.SemaphoreType.DMA
    vmem = pltpu.VMEM
    gathered, new_momentum = pl.pallas_call(
        kernel,
        out_shape=(
            jax.ShapeDtypeStruct((N, N, N, height, width), bf),
            jax.ShapeDtypeStruct((slots, height, width), f4),
        ),
        in_specs=[
            pl.BlockSpec(memory_space=pltpu.SMEM),
            pl.BlockSpec(memory_space=pl.ANY),
            pl.BlockSpec(memory_space=pl.ANY),
            pl.BlockSpec(memory_space=vmem),
        ],
        out_specs=(pl.BlockSpec(memory_space=vmem), pl.BlockSpec(memory_space=vmem)),
        scratch_shapes=[
            vmem((N, N, N, height, width), bf),
            vmem((N, N, HALF, width), f4),
            vmem((N, N, HALF, width), f4),
            vmem((N - 1, N, N, HALF, width), bf),
            vmem((N - 1, N, N, HALF, width), bf),
            vmem((N - 1, N, HALF, width), bf),
            vmem((N - 1, N, HALF, width), bf),
            vmem((N - 1, N, HALF, width), bf),
            vmem((N - 1, N, HALF, width), bf),
            vmem((N, height, width), f4),
            vmem((N, N, N, height, width), bf),
            vmem((2 * N, HALF, width), f4),
            vmem((2 * N, HALF, width), bf),
            vmem((2 * NEAR - 1, HALF, width), bf),
            vmem((HALF, width), bf),
            vmem((FAR - 1, HALF, width), bf),
            vmem((2 * N, HALF, width), bf),
            dma((N * N,)),
            dma((2,)),
            dma((2, (N - 1) * N)),
            dma((2, (N - 1) * N)),
            dma((2, N - 1)),
            dma((2, N - 1)),
            dma((2, N - 1)),
            dma((2, N - 1)),
            dma((2, (N - 1) * (N - 1))),
            dma((2, (N - 1) * (N - 1))),
            dma((2, N - 1)),
            dma((2, N - 1)),
            dma((2, (N - 1) * (N - 1))),
            dma((2, (N - 1) * (N - 1))),
            dma((2 * NEAR - 1,)),
            dma((2 * NEAR - 1,)),
            dma((FAR - 1,)),
            dma((FAR - 1,)),
            dma((2 * NEAR - 1,)),
            dma((2 * NEAR - 1,)),
        ],
        compiler_params=pltpu.CompilerParams(
            collective_id=0, has_side_effects=True, vmem_limit_bytes=32 * 1024 * 1024
        ),
        name="outer_step",
    )(
        table,
        in_hbm(local_params.reshape(N, N, N, height, width)),
        in_hbm(global_params.reshape(N, N, N, height, width)),
        momentum[0],
    )
    factor = math.sqrt(height * lax.axis_size("fsdp") / width)
    update = gathered.reshape(blocks, height, width).astype(f4)
    return (global_params - factor * update, new_momentum[None])


def solution(mesh):
    in_specs = (
        P("island", None, "fsdp", None),
        P(None, "fsdp", None),
        P("island", None, "fsdp", None),
        P(),
    )
    out_specs = (P(None, "fsdp", None), P("island", None, "fsdp", None))
    return jax.shard_map(shards, mesh=mesh, in_specs=in_specs, out_specs=out_specs, check_vma=False)
```

```python
import functools
import math

import jax
import jax.numpy as jnp
from jax import lax
from jax.experimental import pallas as pl
from jax.experimental.pallas import tpu as pltpu
from jax.sharding import PartitionSpec as P

MESH = pl.DeviceIdType.MESH
HIGHEST = lax.Precision.HIGHEST
decay_rate = 0.9
epsilon_norm = 1e-07
coef_a = 3.4445
coef_b = -4.775
coef_c = 2.0315

N = 4
NEAR = 4
FAR = 8
HALF = 64
LOOK_P = 1.0 + decay_rate
LOOK_M = decay_rate * decay_rate


def kernel(
    factor, table, local, globe, mom, newp, newmom,
    lown, xall, r1a, r1b, s2a, s2b, r2a, r2b, look, lookall, gpart, gsend, rnear, fown, rfar, gfull,
    load_sem, g_sem, s1_send, s1_recv, s2_send, s2_recv,
    l_send, l_recv, lf_send, lf_recv, x_send, x_recv, xf_send, xf_recv, n_send, n_recv, f_send, f_recv, a_send, a_recv,
):
    island, fsdp = lax.axis_index("island"), lax.axis_index("fsdp")
    x, y = island // N, island % N
    z, core = fsdp // 2, fsdp % 2
    near = (z % NEAR) * 2 + core

    def at_xy(px, py):
        return (px * N + py, fsdp)

    def x_peer(j):
        return at_xy((x + j) % N, y)

    def y_peer(j):
        return at_xy(x, (y + j) % N)

    def near_peer(q):
        other = (near + q) % (2 * NEAR)
        return (island, ((z // NEAR) * NEAR + other // 2) * 2 + other % 2)

    def far_peer(q):
        return (island, ((z + NEAR * q) % (NEAR * FAR)) * 2 + core)

    barrier = pltpu.get_barrier_semaphore()
    peers = [x_peer(j) for j in range(1, N)] + [y_peer(j) for j in range(1, N)]
    peers += [near_peer(q) for q in range(1, 2 * NEAR)] + [far_peer(q) for q in (1, 2, FAR - 2, FAR - 1)]
    for peer in peers:
        pl.semaphore_signal(barrier, inc=1, device_id=peer, device_id_type=MESH)

    order = [(t, j) for t in (1, 2, 3, 0) for j in (1, 2, 3, 0)]
    loads = {}
    for t, j in order:
        place = ((x + t) % N, (y + j) % N)
        loads[t, j] = pltpu.make_async_copy(local.at[place], lown.at[place], load_sem.at[t * N + j])
        loads[t, j].start()
    load_g = pltpu.make_async_copy(globe, newp, g_sem)
    load_g.start()

    def remote(src, dst, send, recv, peer):
        return pltpu.make_async_remote_copy(
            src_ref=src, dst_ref=dst, send_sem=send, recv_sem=recv, device_id=peer, device_id_type=MESH
        )

    sent = []
    first_a, first_b = {}, {}
    inject = 16.0 * LOOK_M / LOOK_P
    for t, j in order:
        px, py = (x + t) % N, (y + j) % N
        loads[t, j].wait()

        def put(k, _, px=px, py=py):
            block = (px * N + py) * N + k
            scale = table[64 + block].astype(jnp.float32) * inject
            term = lown[px, py, k].astype(jnp.float32) - scale * mom[table[block]]
            lown[px, py, k] = term.astype(jnp.bfloat16)
            return 0

        lax.fori_loop(0, N, put, 0)
    pl.semaphore_wait(barrier, len(peers))
    for t, j in order:
        px, py = (x + t) % N, (y + j) % N
        if j:
            at = (j - 1) * N + t
            copy = remote(
                lown.at[px, py, :, 0:HALF, :], r1a.at[j - 1, px], s1_send.at[0, at], s1_recv.at[0, at], y_peer(j)
            )
            copy.start()
            first_a[t, j] = copy
        if t:
            at = (t - 1) * N + j
            copy = remote(
                lown.at[px, py, :, HALF : 2 * HALF, :], r1b.at[t - 1, py], s1_send.at[1, at], s1_recv.at[1, at], x_peer(t)
            )
            copy.start()
            first_b[t, j] = copy
    sent += list(first_a.values()) + list(first_b.values())
    load_g.wait()

    def line_a(t):
        px = (x + t) % N
        for j in range(1, N):
            first_a[t, j].wait_recv()
        total = lown[px, y, :, 0:HALF, :].astype(jnp.float32)
        for j in range(1, N):
            total = total + r1a[j - 1, px].astype(jnp.float32)
        return N * newp[px, y, :, 0:HALF, :] - total

    def line_b(j):
        py = (y + j) % N
        for t in range(1, N):
            first_b[t, j].wait_recv()
        total = lown[x, py, :, HALF : 2 * HALF, :].astype(jnp.float32)
        for t in range(1, N):
            total = total + r1b[t - 1, py].astype(jnp.float32)
        return N * newp[x, py, :, HALF : 2 * HALF, :] - total

    second = []
    for s in range(1, N):
        s2a[s - 1] = line_a(s).astype(jnp.bfloat16)
        copy_a = remote(s2a.at[s - 1], r2a.at[s - 1], s2_send.at[0, s - 1], s2_recv.at[0, s - 1], x_peer(s))
        copy_a.start()
        s2b[s - 1] = line_b(s).astype(jnp.bfloat16)
        copy_b = remote(s2b.at[s - 1], r2b.at[s - 1], s2_send.at[1, s - 1], s2_recv.at[1, s - 1], y_peer(s))
        copy_b.start()
        second += [copy_a, copy_b]
    look[:, 0:HALF, :] = line_a(0)
    look[:, HALF : 2 * HALF, :] = line_b(0)
    for copy in second:
        copy.wait_recv()
    sent += second
    total_a, total_b = look[:, 0:HALF, :], look[:, HALF : 2 * HALF, :]
    for s in range(N - 1):
        total_a = total_a + r2a[s].astype(jnp.float32)
        total_b = total_b + r2b[s].astype(jnp.float32)
    look[:, 0:HALF, :] = total_a * (LOOK_P / 16.0)
    look[:, HALF : 2 * HALF, :] = total_b * (LOOK_P / 16.0)
    lookall[x, y] = look[...].astype(jnp.bfloat16)

    def gather_own(buf, send, recv):
        copies = []
        for j in range(1, N):
            for way, peer in enumerate((x_peer(j), y_peer(j))):
                copy = remote(buf.at[x, y], buf.at[x, y], send.at[way, j - 1], recv.at[way, j - 1], peer)
                copy.start()
                copies.append(copy)
        return copies

    def gather_forward(buf, direct, send, recv):
        copies = []
        for j in range(1, N):
            for way in range(2):
                direct[(j - 1) * 2 + way].wait_recv()
                for i in range(1, N):
                    at = (j - 1) * (N - 1) + i - 1
                    if way == 0:
                        piece = buf.at[(x - j + N) % N, y, :, 0:HALF, :]
                        copy = remote(piece, piece, send.at[0, at], recv.at[0, at], y_peer(i))
                    else:
                        piece = buf.at[x, (y - j + N) % N, :, HALF : 2 * HALF, :]
                        copy = remote(piece, piece, send.at[1, at], recv.at[1, at], x_peer(i))
                    copy.start()
                    copies.append(copy)
        return copies

    look_direct = gather_own(lookall, l_send, l_recv)
    sent += look_direct

    for k in range(N):
        block = look[k]
        gram = lax.dot_general(
            block, block, (((0,), (0,)), ((), ())), precision=HIGHEST, preferred_element_type=jnp.float32
        )
        gpart[2 * k] = gram[0:HALF]
        gpart[2 * k + 1] = gram[HALF : 2 * HALF]
    gsend[...] = gpart[...].astype(jnp.bfloat16)
    steps = []
    for q in range(1, 2 * NEAR):
        other = (near + q) % (2 * NEAR)
        copy = remote(gsend.at[other], rnear.at[q - 1], n_send.at[q - 1], n_recv.at[q - 1], near_peer(q))
        copy.start()
        steps.append(copy)
    for copy in steps:
        copy.wait_recv()
    sent += steps
    mine = gpart[near]
    for q in range(2 * NEAR - 1):
        mine = mine + rnear[q].astype(jnp.float32)
    fown[...] = mine.astype(jnp.bfloat16)
    steps = []
    for slot, q in enumerate((2, FAR - 2, 1, FAR - 1)):
        copy = remote(fown, rfar.at[slot], f_send.at[slot], f_recv.at[slot], far_peer(q))
        copy.start()
        steps.append(copy)
    steps[0].wait_recv()
    for slot, q in ((4, 2), (5, 1)):
        copy = remote(rfar.at[0], rfar.at[slot], f_send.at[slot], f_recv.at[slot], far_peer(q))
        copy.start()
        steps.append(copy)
    steps[1].wait_recv()
    copy = remote(rfar.at[1], rfar.at[6], f_send.at[6], f_recv.at[6], far_peer(FAR - 1))
    copy.start()
    steps.append(copy)
    look_forward = gather_forward(lookall, look_direct, lf_send, lf_recv)
    sent += look_forward
    for copy in steps[2:]:
        copy.wait_recv()
    sent += steps
    for q in range(FAR - 1):
        mine = mine + rfar[q].astype(jnp.float32)
    gfull[near] = mine.astype(jnp.bfloat16)
    steps = []
    for q in range(1, 2 * NEAR):
        copy = remote(gfull.at[near], gfull.at[near], a_send.at[q - 1], a_recv.at[q - 1], near_peer(q))
        copy.start()
        steps.append(copy)
    for copy in steps:
        copy.wait_recv()
    sent += steps

    def mm(left, right):
        return jnp.dot(left, right, precision=HIGHEST, preferred_element_type=jnp.float32)

    rows = lax.broadcasted_iota(jnp.int32, (2 * HALF, 2 * HALF), 0)
    cols = lax.broadcasted_iota(jnp.int32, (2 * HALF, 2 * HALF), 1)
    eye = jnp.where(rows == cols, 1.0, 0.0).astype(jnp.float32)
    grams, scales = [], []
    for k in range(N):
        gram = gfull[2 * k : 2 * k + 2].astype(jnp.float32).reshape(2 * HALF, 2 * HALF)
        squares = jnp.sum(jnp.sum(gram * eye, axis=1, keepdims=True), axis=0, keepdims=True)
        scale = 1.0 / (jnp.sqrt(squares) + epsilon_norm)
        grams.append(gram * scale * scale)
        scales.append(scale)
    mults = None
    for step in range(3):
        squared = [mm(gram, gram) for gram in grams]
        polys = [coef_a * eye + coef_b * gram + coef_c * square for gram, square in zip(grams, squared)]
        if step < 2:
            inner = [mm(poly, gram) for poly, gram in zip(polys, grams)]
            grams = [mm(poly, part) for poly, part in zip(polys, inner)]
        mults = polys if mults is None else [mm(mult, poly) for mult, poly in zip(mults, polys)]
    for k in range(N):
        xall[x, y, k] = mm(look[k], mults[k] * scales[k]).astype(jnp.bfloat16)

    def use(px, py):
        newp[px, py] = newp[px, py] - factor * xall[px, py].astype(jnp.float32)

    x_direct = gather_own(xall, x_send, x_recv)
    sent += x_direct

    for copy in look_forward:
        copy.wait_recv()

    for s in range(newmom.shape[0]):
        block = table[128 + s]
        used = table[136 + s]
        old = mom[s]
        seen = lookall[block // 16, (block // N) % N, block % N].astype(jnp.float32)
        fresh = decay_rate * old + (seen - LOOK_M * old) * (1.0 / LOOK_P)
        newmom[s] = jnp.where(used > 0, fresh, old)

    use(x, y)
    x_forward = gather_forward(xall, x_direct, xf_send, xf_recv)
    sent += x_forward
    for j in range(1, N):
        use((x - j + N) % N, y)
        use(x, (y - j + N) % N)
    for a in range(1, N):
        for b in range(1, N):
            x_forward[((a - 1) * 2) * (N - 1) + b - 1].wait_recv()
            x_forward[((b - 1) * 2 + 1) * (N - 1) + a - 1].wait_recv()
            use((x - a + N) % N, (y - b + N) % N)
    for copy in sent:
        copy.wait_send()


def shards(local_params, global_params, momentum, owners):
    my_island = lax.axis_index("island")
    blocks, height, width = global_params.shape
    slots = momentum.shape[1]
    owner = owners[:, 0]
    ids = jnp.arange(blocks, dtype=jnp.int32)
    earlier = (owner[None, :] == owner[:, None]) & (ids[None, :] < ids[:, None])
    position = jnp.sum(earlier.astype(jnp.int32), axis=1)
    own = owner == my_island
    route = jnp.where(own, position, 0)
    hit = own[None, :] & (position[None, :] == jnp.arange(8, dtype=jnp.int32)[:, None])
    holds = jnp.sum(jnp.where(hit, ids[None, :], 0), axis=1)
    used = jnp.sum(hit.astype(jnp.int32), axis=1)
    table = jnp.concatenate([route, own.astype(jnp.int32), holds, used])

    def in_hbm(array):
        return pltpu.with_memory_space_constraint(array, pltpu.HBM)

    factor = math.sqrt(height * lax.axis_size("fsdp") / width)
    bf, f4 = jnp.bfloat16, jnp.float32
    dma = pltpu.SemaphoreType.DMA
    vmem = pltpu.VMEM
    new_params, new_momentum = pl.pallas_call(
        functools.partial(kernel, factor),
        out_shape=(
            jax.ShapeDtypeStruct((N, N, N, height, width), f4),
            jax.ShapeDtypeStruct((slots, height, width), f4),
        ),
        in_specs=[
            pl.BlockSpec(memory_space=pltpu.SMEM),
            pl.BlockSpec(memory_space=pl.ANY),
            pl.BlockSpec(memory_space=pl.ANY),
            pl.BlockSpec(memory_space=vmem),
        ],
        out_specs=(pl.BlockSpec(memory_space=vmem), pl.BlockSpec(memory_space=vmem)),
        scratch_shapes=[
            vmem((N, N, N, height, width), bf),
            vmem((N, N, N, height, width), bf),
            vmem((N - 1, N, N, HALF, width), bf),
            vmem((N - 1, N, N, HALF, width), bf),
            vmem((N - 1, N, HALF, width), bf),
            vmem((N - 1, N, HALF, width), bf),
            vmem((N - 1, N, HALF, width), bf),
            vmem((N - 1, N, HALF, width), bf),
            vmem((N, height, width), f4),
            vmem((N, N, N, height, width), bf),
            vmem((2 * N, HALF, width), f4),
            vmem((2 * N, HALF, width), bf),
            vmem((2 * NEAR - 1, HALF, width), bf),
            vmem((HALF, width), bf),
            vmem((FAR - 1, HALF, width), bf),
            vmem((2 * N, HALF, width), bf),
            dma((N * N,)),
            dma,
            dma((2, (N - 1) * N)),
            dma((2, (N - 1) * N)),
            dma((2, N - 1)),
            dma((2, N - 1)),
            dma((2, N - 1)),
            dma((2, N - 1)),
            dma((2, (N - 1) * (N - 1))),
            dma((2, (N - 1) * (N - 1))),
            dma((2, N - 1)),
            dma((2, N - 1)),
            dma((2, (N - 1) * (N - 1))),
            dma((2, (N - 1) * (N - 1))),
            dma((2 * NEAR - 1,)),
            dma((2 * NEAR - 1,)),
            dma((FAR - 1,)),
            dma((FAR - 1,)),
            dma((2 * NEAR - 1,)),
            dma((2 * NEAR - 1,)),
        ],
        compiler_params=pltpu.CompilerParams(
            collective_id=0, has_side_effects=True, vmem_limit_bytes=32 * 1024 * 1024
        ),
        name="outer_step",
    )(
        table,
        in_hbm(local_params.reshape(N, N, N, height, width)),
        in_hbm(global_params.reshape(N, N, N, height, width)),
        momentum[0],
    )
    return (new_params.reshape(blocks, height, width), new_momentum[None])


def solution(mesh):
    in_specs = (
        P("island", None, "fsdp", None),
        P(None, "fsdp", None),
        P("island", None, "fsdp", None),
        P(),
    )
    out_specs = (P(None, "fsdp", None), P("island", None, "fsdp", None))
    return jax.shard_map(shards, mesh=mesh, in_specs=in_specs, out_specs=out_specs, check_vma=False)
```
